32 devices in a mesh: lat: 8 (over z, y), lon: 4 (over x, core).
Axes of the slice: x: 2, y: 2, z: 4, core: 2. Of those that a mesh axis runs over, the one named last changes fastest.
Arguments:
- field_in: bfloat16 [64, 1440, 384], P('lat', 'lon'), may hold values from -3 to 3
- cotangent: bfloat16 [64, 1440, 384], P('lat', 'lon'), may hold values from -3 to 3
- legendre: bfloat16 [256, 360, 64], P(('lat', 'lon')), may hold values from -0.5 to 0.5
- spectral_gain: float32 [360, 384], replicated, may hold values from -5 to 5
- disco_kernel: bfloat16 [64, 17, 3], replicated, may hold values from -4 to 4
- extents: int32 [64], replicated, may hold values from 1 to 8, as said below
- mixing: bfloat16 [384, 384], replicated, may hold values from -0.3125 to 0.3125
Outputs:
- layer_out: bfloat16 [64, 1440, 384], P('lat', 'lon')
- grad_in: bfloat16 [64, 1440, 384], P('lat', 'lon')
The draws below stay inside these ranges and needn't reach their ends.
Inputs may be any that keep to these rules, and one draw needn't show every extreme that they name: extents[i] is row i's window half-width; the two polar rows have 8.
All inputs are finite; a program needn't handle non-finite values.
Results may differ from the reference program's by a relative error of at most 0.011.
Values may be sent and summed in bfloat16 or wider, within the bound.
A program may use at most 128 MiB of HBM per device.

```python
import math
import jax
import jax.numpy as jnp
from jax import lax

C = 384
NLON = 1440
MODES = 256
DEGREES = 360
MAX_EXT = 8
NLAT = 64
WIN = 17


def draw_extents(key, part):
    key = jax.random.fold_in(key, 7)
    row_numbers = jnp.arange(NLAT, dtype=jnp.int32)
    distance = jnp.minimum(row_numbers, NLAT - 1 - row_numbers)
    polar_zone = max(NLAT // 8, 1)
    widening = MAX_EXT - distance * MAX_EXT // polar_zone
    jitter = jax.random.randint(key, (NLAT,), -1, 2, dtype=jnp.int32)
    result = jnp.clip(widening + jitter, 1, MAX_EXT)
    result = jnp.where(distance == 0, MAX_EXT, result)
    return result.astype(jnp.int32)


def block_levels(rng, shape, shards, smallest, high):
    def one(axis_at, shards_of):
        heights = jax.random.uniform(jax.random.fold_in(jax.random.fold_in(rng, 6), axis_at), (shards_of,), jnp.float32, smallest / len(shards), high / len(shards))
        return jnp.repeat(jnp.exp(heights), shape[axis_at] // shards_of).reshape((-1,) + (1,) * (len(shape) - axis_at - 1))

    gain = one(*shards[0])
    for cut in shards[1:]:
        gain = gain * one(*cut)
    return gain


def bell_draw(key, shape, width, most, split=(), held_as=jnp.bfloat16):
    values = jax.random.normal(key, shape, jnp.float32) * width
    if len(split) > 0:
        values = block_levels(key, shape, split, -0.22, 0.18) * values
    return jnp.clip(values, min=-most, max=most).astype(held_as)


def setup_inputs(seed: int = 0) -> dict:
    splits = jax.random.split(jax.random.key(seed), 8)
    return {
        "field_in": bell_draw(splits[0], (NLAT, NLON, C), 1.0, 3.0, ((0, 8), (1, 4))),
        "cotangent": bell_draw(splits[1], (NLAT, NLON, C), 1.0, 3.0, ((0, 8), (1, 4))),
        "legendre": bell_draw(splits[2], (MODES, DEGREES, NLAT), ((NLAT * DEGREES) ** 0.5) ** -0.5, 0.5, ((0, 32),)),
        "spectral_gain": bell_draw(splits[3], (DEGREES, C), 1.0, 5.0, (), jnp.float32),
        "disco_kernel": bell_draw(splits[4], (NLAT, WIN, 3), 0.3, 4.0),
        "extents": draw_extents(jax.random.fold_in(splits[7], 71), 0),
        "mixing": bell_draw(splits[6], (C, C), C ** -0.5, 0.3125),
    }


def masked_kernel(disco_kernel, extents):
    offsets = jnp.arange(2 * MAX_EXT + 1, dtype=jnp.int32) - MAX_EXT
    inside = jnp.abs(offsets)[None, :] <= extents[:, None]
    return jnp.where(inside[:, :, None], disco_kernel, jnp.zeros_like(disco_kernel))

def zonal_tables(mode_numbers, lon_numbers):
    phase = mode_numbers[:, None] * lon_numbers[None, :] % NLON
    angle = phase.astype(jnp.float32) * (2.0 * math.pi / NLON)
    return (jnp.cos(angle).astype(jnp.bfloat16), (-jnp.sin(angle)).astype(jnp.bfloat16))

def band_matrices(kernel):
    offsets = jnp.arange(2 * MAX_EXT + 1, dtype=jnp.int32) - MAX_EXT
    target = jnp.arange(NLAT, dtype=jnp.int32)[:, None] + offsets[None, :]
    onehot = (target[:, :, None] == jnp.arange(NLAT, dtype=jnp.int32)[None, None, :]).astype(jnp.float32)
    return jnp.einsum('iwk,iwj->kij', kernel.astype(jnp.float32), onehot).astype(jnp.bfloat16)

def disco_forward(field, matrices):
    total = jnp.zeros((NLAT, NLON * C), jnp.float32)
    for shift in range(3):
        moved = jnp.roll(field, 1 - shift, axis=1).reshape(NLAT, NLON * C)
        total = total + jnp.dot(matrices[shift], moved, preferred_element_type=jnp.float32)
    return total.reshape(NLAT, NLON, C)

def disco_adjoint(field, matrices):
    total = jnp.zeros((NLAT, NLON * C), jnp.float32)
    for shift in range(3):
        moved = jnp.roll(field, shift - 1, axis=1).reshape(NLAT, NLON * C)
        total = total + jnp.dot(jnp.transpose(matrices[shift]), moved, preferred_element_type=jnp.float32)
    return total.reshape(NLAT, NLON, C)

def analysis(field, scale):
    cosines, sines = zonal_tables(jnp.arange(MODES, dtype=jnp.int32), jnp.arange(NLON, dtype=jnp.int32))
    flat = jnp.transpose(field, (1, 0, 2)).reshape(NLON, NLAT * C)
    real_part = jnp.dot(cosines, flat, preferred_element_type=jnp.float32) * scale
    imag_part = jnp.dot(sines, flat, preferred_element_type=jnp.float32) * scale
    stacked = jnp.stack([real_part, imag_part], axis=1)
    return stacked.reshape(MODES, 2, NLAT, C).astype(jnp.bfloat16)

def legendre_chain(coeffs, legendre, spectral_gain):

    def one_mode(operands):
        matrix, values = operands
        stacked = jnp.transpose(values, (1, 0, 2)).reshape(NLAT, 2 * C)
        degree_sums = jnp.dot(matrix, stacked, preferred_element_type=jnp.float32).reshape(DEGREES, 2, C)
        filtered = (degree_sums * spectral_gain[:, None, :]).astype(jnp.bfloat16)
        lat_values = jnp.dot(jnp.transpose(matrix), filtered.reshape(DEGREES, 2 * C), preferred_element_type=jnp.float32)
        return jnp.transpose(lat_values.reshape(NLAT, 2, C), (1, 0, 2)).astype(jnp.bfloat16)
    return lax.map(one_mode, (legendre, coeffs))

def synthesis(coeffs, scale):
    cosines, sines = zonal_tables(jnp.arange(MODES, dtype=jnp.int32), jnp.arange(NLON, dtype=jnp.int32))
    real_part = coeffs[:, 0].reshape(MODES, NLAT * C)
    imag_part = coeffs[:, 1].reshape(MODES, NLAT * C)
    total = jnp.dot(jnp.transpose(cosines), real_part, preferred_element_type=jnp.float32)
    total = total + jnp.dot(jnp.transpose(sines), imag_part, preferred_element_type=jnp.float32)
    return jnp.transpose(total.reshape(NLON, NLAT, C), (1, 0, 2)) * scale

def spectral(field, legendre, spectral_gain, first_scale, second_scale):
    coeffs = legendre_chain(analysis(field, first_scale), legendre, spectral_gain)
    return synthesis(coeffs, second_scale)

def gelu_slope(values):
    return jax.vjp(jax.nn.gelu, values)[1](jnp.ones_like(values))[0]

def reference(field_in, cotangent, legendre, spectral_gain, disco_kernel, extents, mixing):
    matrices = band_matrices(masked_kernel(disco_kernel, extents))
    local_sum = disco_forward(field_in, matrices).astype(jnp.bfloat16)
    local_branch = jnp.dot(local_sum.reshape(NLAT * NLON, C), mixing, preferred_element_type=jnp.float32).reshape(NLAT, NLON, C)
    pre_act = local_branch + spectral(field_in, legendre, spectral_gain, 1.0 / math.sqrt(NLON), 1.0 / math.sqrt(MODES))
    layer_out = (field_in.astype(jnp.float32) + jax.nn.gelu(pre_act)).astype(jnp.bfloat16)
    upstream = (cotangent.astype(jnp.float32) * gelu_slope(pre_act)).astype(jnp.bfloat16)
    local_back = jnp.dot(upstream.reshape(NLAT * NLON, C), jnp.transpose(mixing), preferred_element_type=jnp.float32)
    local_back = local_back.astype(jnp.bfloat16).reshape(NLAT, NLON, C)
    grad_in = cotangent.astype(jnp.float32) + disco_adjoint(local_back, matrices)
    grad_in = grad_in + spectral(upstream, legendre, spectral_gain, 1.0 / math.sqrt(MODES), 1.0 / math.sqrt(NLON))
    return (layer_out, grad_in.astype(jnp.bfloat16))
```

```python
import functools
import math

import jax
import jax.numpy as jnp
from jax import lax
from jax.sharding import PartitionSpec as P

NLON = 1440
MODES = 256
MAX_EXT = 8


def extended(cells, sides, width, closed):
    for axis, dim in sides:
        count = lax.axis_size(axis)
        ends = count if closed else count - 1
        head = lax.slice_in_dim(cells, 0, width, axis=dim)
        tail = lax.slice_in_dim(cells, cells.shape[dim] - width, cells.shape[dim], axis=dim)
        cells = jnp.concatenate(
            [
                lax.ppermute(tail, axis, [(i, (i + 1) % count) for i in range(ends)]),
                cells,
                lax.ppermute(head, axis, [((i + 1) % count, i) for i in range(ends)]),
            ],
            axis=dim,
        )
    return cells


def masked_kernel(disco_kernel, extents):
    offsets = jnp.arange(2 * MAX_EXT + 1, dtype=jnp.int32) - MAX_EXT
    inside = jnp.abs(offsets)[None, :] <= extents[:, None]
    return jnp.where(inside[:, :, None], disco_kernel, jnp.zeros_like(disco_kernel))


def zonal_tables(mode_numbers, lon_numbers):
    phase = mode_numbers[:, None] * lon_numbers[None, :] % NLON
    angle = phase.astype(jnp.float32) * (2.0 * math.pi / NLON)
    return (jnp.cos(angle).astype(jnp.bfloat16), (-jnp.sin(angle)).astype(jnp.bfloat16))


def swap(values, distance):
    count = lax.axis_size("lon")
    return lax.ppermute(values, "lon", [(i, i ^ distance) for i in range(count)])


def group_tables(lat_count, lon_count, lon_width):
    per_lon = MODES // lon_count
    per_device = per_lon // lat_count
    me = lax.axis_index("lon")
    lon_numbers = me * lon_width + jnp.arange(lon_width, dtype=jnp.int32)
    order = jnp.arange(lon_count, dtype=jnp.int32) ^ me
    inner = jnp.arange(per_lon, dtype=jnp.int32)
    base = (inner // per_device) * (lon_count * per_device) + inner % per_device
    modes = (order[:, None] * per_device + base[None, :]).reshape(-1)
    return tuple(
        table.reshape(lon_count, per_lon, lon_width)
        for table in zonal_tables(modes, lon_numbers)
    )


def pick(table, groups):
    return jnp.concatenate([table[g] for g in groups], axis=0)


def reduce_lon(field, table, scale):
    lon_count, per_lon, _ = table.shape
    held = list(range(lon_count))
    distance = 1
    sums = {}

    def partial(groups):
        got = jnp.einsum("rp,ipc->ric", pick(table, groups), field, preferred_element_type=jnp.float32)
        return (got * scale).reshape((len(groups), per_lon) + got.shape[1:])

    current = None
    while distance < lon_count:
        keep = [g for g in held if not g & distance]
        away = [g for g in held if g & distance]
        if current is None:
            sent = swap(partial(away).astype(jnp.bfloat16), distance)
            kept = partial(keep)
        else:
            at = {g: n for n, g in enumerate(held)}
            sent = swap(jnp.stack([current[at[g]] for g in away]).astype(jnp.bfloat16), distance)
            kept = jnp.stack([current[at[g]] for g in keep])
        current = kept + sent.astype(jnp.float32)
        held = keep
        distance *= 2
    if current is None:
        current = partial(held)
    return current[0].astype(jnp.bfloat16)


def legendre_chain(zonal, legendre, spectral_gain):
    moved = lax.all_to_all(zonal, "lat", split_axis=0, concat_axis=1, tiled=True)
    degree_sums = jnp.einsum("sln,snc->slc", legendre, moved, preferred_element_type=jnp.float32)
    filtered = (degree_sums * spectral_gain[None]).astype(jnp.bfloat16)
    lat_values = jnp.einsum("sln,slc->snc", legendre, filtered, preferred_element_type=jnp.float32)
    return lax.all_to_all(
        lat_values.astype(jnp.bfloat16), "lat", split_axis=1, concat_axis=0, tiled=True
    )


def spread_lon(coeffs, table):
    lon_count = table.shape[0]
    pieces = [coeffs]
    groups = [0]
    distance = lon_count // 2
    total = None
    while distance >= 1:
        packed = pieces[0] if len(pieces) == 1 else jnp.concatenate(pieces, axis=0)
        got = swap(packed, distance)
        pieces = [packed, got]
        groups = groups + [g ^ distance for g in groups]
        distance //= 2
    packed = jnp.concatenate(pieces, axis=0) if len(pieces) > 1 else pieces[0]
    return jnp.einsum("rp,ric->ipc", pick(table, groups), packed, preferred_element_type=jnp.float32)


def spectral(field, tables, legendre, spectral_gain, first_scale, second_scale):
    parts = [reduce_lon(field, table, first_scale) for table in tables]
    parts = [legendre_chain(part, legendre, spectral_gain) for part in parts]
    total = spread_lon(parts[0], tables[0]) + spread_lon(parts[1], tables[1])
    return total * second_scale


def near_matrices(disco_kernel, extents, lat_rows, depth):
    kernel_all = masked_kernel(disco_kernel, extents)
    kernel_own = lax.dynamic_slice_in_dim(
        kernel_all, lax.axis_index("lat") * lat_rows, lat_rows, 0
    )
    span = lat_rows + 2 * depth
    taps = (
        jnp.arange(span, dtype=jnp.int32)[None, :]
        - depth
        - jnp.arange(lat_rows, dtype=jnp.int32)[:, None]
        + MAX_EXT
    )
    picked = (
        jnp.arange(2 * MAX_EXT + 1, dtype=jnp.int32)[None, None, :] == taps[:, :, None]
    ).astype(jnp.float32)
    return jnp.einsum("iwk,ihw->ihk", kernel_own.astype(jnp.float32), picked).astype(jnp.bfloat16)


def window_sum(field, matrices, depth):
    padded = extended(extended(field, (("lat", 0),), depth, False), (("lon", 1),), 1, True)
    lon_width = field.shape[1]
    total = jnp.zeros(field.shape, jnp.float32)
    for shift in range(3):
        total = total + jnp.einsum(
            "ih,hpc->ipc",
            matrices[:, :, shift],
            padded[:, shift : shift + lon_width],
            preferred_element_type=jnp.float32,
        )
    return total


def window_sum_back(field, matrices, depth):
    lat_rows, lon_width, _ = field.shape
    padded = extended(field, (("lon", 1),), 1, True)

    def rows_sum(first, last):
        total = None
        for shift in range(3):
            term = jnp.einsum(
                "ij,ipc->jpc",
                matrices[:, first:last, shift],
                padded[:, 2 - shift : 2 - shift + lon_width],
                preferred_element_type=jnp.float32,
            )
            total = term if total is None else total + term
        return total

    count = lax.axis_size("lat")
    up = [(i, i + 1) for i in range(count - 1)]
    down = [(i + 1, i) for i in range(count - 1)]
    before = rows_sum(0, depth).astype(jnp.bfloat16)
    after = rows_sum(depth + lat_rows, lat_rows + 2 * depth).astype(jnp.bfloat16)
    from_below = lax.ppermute(after, "lat", up)
    from_above = lax.ppermute(before, "lat", down)
    own = rows_sum(depth, depth + lat_rows)
    pad = ((0, lat_rows - depth), (0, 0), (0, 0))
    pad_up = ((lat_rows - depth, 0), (0, 0), (0, 0))
    return (
        own
        + jnp.pad(from_below, pad).astype(jnp.float32)
        + jnp.pad(from_above, pad_up).astype(jnp.float32)
    )


def gelu_slope(values):
    return jax.vjp(jax.nn.gelu, values)[1](jnp.ones_like(values))[0]


def layer(depth, field_in, cotangent, legendre, spectral_gain, disco_kernel, extents, mixing):
    lat_rows, lon_width, channels = field_in.shape
    tables = group_tables(lax.axis_size("lat"), lax.axis_size("lon"), lon_width)
    matrices = near_matrices(disco_kernel, extents, lat_rows, depth)
    local_sum = window_sum(field_in, matrices, depth).astype(jnp.bfloat16)
    local_branch = jnp.dot(
        local_sum.reshape(lat_rows * lon_width, channels),
        mixing,
        preferred_element_type=jnp.float32,
    ).reshape(lat_rows, lon_width, channels)
    pre_act = local_branch + spectral(
        field_in, tables, legendre, spectral_gain, 1.0 / math.sqrt(NLON), 1.0 / math.sqrt(MODES)
    )
    layer_out = (field_in.astype(jnp.float32) + jax.nn.gelu(pre_act)).astype(jnp.bfloat16)
    upstream = (cotangent.astype(jnp.float32) * gelu_slope(pre_act)).astype(jnp.bfloat16)
    local_back = jnp.dot(
        upstream.reshape(lat_rows * lon_width, channels),
        jnp.transpose(mixing),
        preferred_element_type=jnp.float32,
    )
    local_back = local_back.astype(jnp.bfloat16).reshape(lat_rows, lon_width, channels)
    grad_in = cotangent.astype(jnp.float32) + window_sum_back(local_back, matrices, depth)
    grad_in = grad_in + spectral(
        upstream, tables, legendre, spectral_gain, 1.0 / math.sqrt(MODES), 1.0 / math.sqrt(NLON)
    )
    return (layer_out, grad_in.astype(jnp.bfloat16))


NEAR = 2


def body(field_in, cotangent, legendre, spectral_gain, disco_kernel, extents, mixing):
    lat_rows = field_in.shape[0]
    rows = jnp.arange(extents.shape[0], dtype=jnp.int32)
    first = rows // lat_rows * lat_rows
    above = first - jnp.maximum(rows - extents, 0)
    below = jnp.minimum(rows + extents, extents.shape[0] - 1) - (first + lat_rows - 1)
    reach = jnp.max(jnp.maximum(above, below))
    return lax.cond(
        reach <= NEAR,
        functools.partial(layer, NEAR),
        functools.partial(layer, MAX_EXT),
        field_in,
        cotangent,
        legendre,
        spectral_gain,
        disco_kernel,
        extents,
        mixing,
    )


def solution(mesh):
    in_specs = (
        P("lat", "lon", None),
        P("lat", "lon", None),
        P(("lat", "lon"), None, None),
        P(),
        P(),
        P(),
        P(),
    )
    out_specs = (P("lat", "lon", None), P("lat", "lon", None))
    return jax.shard_map(body, mesh=mesh, in_specs=in_specs, out_specs=out_specs, check_vma=False)
```

```python
import functools
import math

import jax
import jax.numpy as jnp
from jax import lax
from jax.experimental import pallas as pl
from jax.experimental.pallas import tpu as pltpu
from jax.sharding import PartitionSpec as P

NLON = 1440
MODES = 256
MAX_EXT = 8


def extended(cells, sides, width, closed):
    for axis, dim in sides:
        count = lax.axis_size(axis)
        ends = count if closed else count - 1
        head = lax.slice_in_dim(cells, 0, width, axis=dim)
        tail = lax.slice_in_dim(cells, cells.shape[dim] - width, cells.shape[dim], axis=dim)
        cells = jnp.concatenate(
            [
                lax.ppermute(tail, axis, [(i, (i + 1) % count) for i in range(ends)]),
                cells,
                lax.ppermute(head, axis, [((i + 1) % count, i) for i in range(ends)]),
            ],
            axis=dim,
        )
    return cells


def masked_kernel(disco_kernel, extents):
    offsets = jnp.arange(2 * MAX_EXT + 1, dtype=jnp.int32) - MAX_EXT
    inside = jnp.abs(offsets)[None, :] <= extents[:, None]
    return jnp.where(inside[:, :, None], disco_kernel, jnp.zeros_like(disco_kernel))


def zonal_tables(mode_numbers, lon_numbers):
    phase = mode_numbers[:, None] * lon_numbers[None, :] % NLON
    angle = phase.astype(jnp.float32) * (2.0 * math.pi / NLON)
    return (jnp.cos(angle).astype(jnp.bfloat16), (-jnp.sin(angle)).astype(jnp.bfloat16))


MESH = pl.DeviceIdType.MESH
GROUP_FLIPS = (0, 2, 1, 3)


def chunk_count(per_device):
    return 2 if per_device % 2 == 0 else 1


def zonal_table(lat_count, lon_count, lon_width):
    per_device = MODES // lon_count // lat_count
    chunks = chunk_count(per_device)
    width = per_device // chunks
    me = lax.axis_index("lon")
    lon_numbers = me * lon_width + jnp.arange(lon_width, dtype=jnp.int32)
    groups = jnp.array(GROUP_FLIPS, jnp.int32) ^ me
    owners = jnp.arange(lat_count, dtype=jnp.int32)
    modes = (
        (owners[None, None, :, None] * lon_count + groups[None, :, None, None]) * per_device
        + jnp.arange(chunks, dtype=jnp.int32)[:, None, None, None] * width
        + jnp.arange(width, dtype=jnp.int32)[None, None, None, :]
    ).reshape(-1)
    cosines, sines = zonal_tables(modes, lon_numbers)
    return jnp.stack([cosines, sines], axis=1).reshape(2 * MODES, lon_width)


def chain_kernel(
    lat_count, chunks,
    part_ref, low_ref, high_ref, gain_ref, coef_ref,
    near_buf, far_send, far_buf, own_buf, zonal_buf, value_buf,
    near_sems, far_sems, out_sems, back_sems, edge_sems,
):
    lat = lax.axis_index("lat")
    lon = lax.axis_index("lon")
    near = {"lon": lon ^ 1}
    far = {"lon": lon ^ 2}
    width = part_ref.shape[3]
    rows = part_ref.shape[4]
    channels = part_ref.shape[5]
    degrees = gain_ref.shape[0]

    def peer(step):
        return lax.rem(lat + step, lat_count)

    barrier = pltpu.get_barrier_semaphore()
    pl.semaphore_signal(barrier, inc=1, device_id=near, device_id_type=MESH)
    pl.semaphore_signal(barrier, inc=1, device_id=far, device_id_type=MESH)

    @pl.loop(1, lat_count)
    def _(step):
        pl.semaphore_signal(barrier, inc=1, device_id={"lat": peer(step)}, device_id_type=MESH)

    pl.semaphore_wait(barrier, lat_count + 1)

    def send(src, dst, sems, index, target):
        return pltpu.make_async_remote_copy(
            src_ref=src,
            dst_ref=dst,
            send_sem=sems.at[(0,) + index],
            recv_sem=sems.at[(1,) + index],
            device_id=target,
            device_id_type=MESH,
        )

    def near_copy(k):
        return send(part_ref.at[k, pl.ds(2, 2)], near_buf.at[k], near_sems, (k,), near)

    def far_copy(k):
        return send(far_send.at[k], far_buf.at[k], far_sems, (k,), far)

    def out_copy(k, step):
        return send(
            own_buf.at[k, peer(step)], zonal_buf.at[k, lat], out_sems, (k, step), {"lat": peer(step)}
        )

    def back_copy(k, step):
        return send(
            value_buf.at[k, peer(step)], coef_ref.at[k, 0, lat], back_sems, (k, step), {"lat": peer(step)}
        )

    def edge_copies(k):
        return (
            send(coef_ref.at[k, 0], coef_ref.at[k, 1], edge_sems, (k, 0), far),
            send(coef_ref.at[k, 0], coef_ref.at[k, 2], edge_sems, (k, 1), near),
            send(coef_ref.at[k, 1], coef_ref.at[k, 3], edge_sems, (k, 2), near),
        )

    for k in range(chunks):
        near_copy(k).start()
    for k in range(chunks):
        near_copy(k).wait_recv()

        @pl.loop(0, lat_count)
        def _(owner):
            got = near_buf[k, 1, owner].astype(jnp.float32)
            far_send[k, owner] = (part_ref[k, 1, owner].astype(jnp.float32) + got).astype(jnp.bfloat16)

        far_copy(k).start()
    for k in range(chunks):
        far_copy(k).wait_recv()

        @pl.loop(0, lat_count)
        def _(owner):
            total = part_ref[k, 0, owner].astype(jnp.float32) + near_buf[k, 0, owner].astype(jnp.float32)
            own_buf[k, owner] = (total + far_buf[k, owner].astype(jnp.float32)).astype(jnp.bfloat16)

        @pl.loop(1, lat_count)
        def _(step):
            out_copy(k, step).start()

        zonal_buf[k, lat] = own_buf[k, lat]
    for k in range(chunks):
        @pl.loop(1, lat_count)
        def _(step):
            out_copy(k, step).wait_recv()

        @pl.loop(0, width)
        def _(mode):
            fields = zonal_buf[k, :, mode].reshape(lat_count * rows, channels)
            sums = jnp.dot(low_ref[k * width + mode], fields, preferred_element_type=jnp.float32)
            kept = sums.reshape(2, degrees, channels) * gain_ref[...][None]
            values = jnp.dot(
                high_ref[k * width + mode],
                kept.reshape(2 * degrees, channels).astype(jnp.bfloat16),
                preferred_element_type=jnp.float32,
            )
            value_buf[k, :, mode] = values.astype(jnp.bfloat16).reshape(lat_count, rows, channels)

        @pl.loop(1, lat_count)
        def _(step):
            back_copy(k, step).start()

        coef_ref[k, 0, lat] = value_buf[k, lat]
    for k in range(chunks):
        @pl.loop(1, lat_count)
        def _(step):
            back_copy(k, step).wait_recv()

        first, second, _third = edge_copies(k)
        first.start()
        second.start()
    for k in range(chunks):
        first, second, third = edge_copies(k)
        first.wait_recv()
        third.start()
    for k in range(chunks):
        first, second, third = edge_copies(k)
        second.wait_recv()
        third.wait_recv()
        first.wait_send()
        second.wait_send()
        third.wait_send()
        near_copy(k).wait_send()
        far_copy(k).wait_send()

        @pl.loop(1, lat_count)
        def _(step):
            out_copy(k, step).wait_send()
            back_copy(k, step).wait_send()


def filter_chain(partials, low, high, spectral_gain):
    chunks, groups, lat_count, width, rows, channels = partials.shape
    block = (chunks, lat_count, width, rows, channels)
    whole = pl.BlockSpec(memory_space=pltpu.VMEM)
    modes = chunks * width
    return pl.pallas_call(
        functools.partial(chain_kernel, lat_count, chunks),
        out_shape=jax.ShapeDtypeStruct(partials.shape, jnp.bfloat16),
        in_specs=[whole] * 4,
        out_specs=whole,
        scratch_shapes=[
            pltpu.VMEM((chunks, 2, lat_count, width, rows, channels), jnp.bfloat16),
            pltpu.VMEM(block, jnp.bfloat16),
            pltpu.VMEM(block, jnp.bfloat16),
            pltpu.VMEM(block, jnp.bfloat16),
            pltpu.VMEM(block, jnp.bfloat16),
            pltpu.VMEM(block, jnp.bfloat16),
            pltpu.SemaphoreType.DMA((2, chunks)),
            pltpu.SemaphoreType.DMA((2, chunks)),
            pltpu.SemaphoreType.DMA((2, chunks, lat_count)),
            pltpu.SemaphoreType.DMA((2, chunks, lat_count)),
            pltpu.SemaphoreType.DMA((2, chunks, 3)),
        ],
        compiler_params=pltpu.CompilerParams(
            collective_id=0, has_side_effects=True, vmem_limit_bytes=40 * 1024 * 1024
        ),
        cost_estimate=pl.CostEstimate(
            flops=modes * 4 * low.shape[1] * low.shape[2] * channels,
            bytes_accessed=8 * partials.size,
            transcendentals=0,
        ),
    )(partials, low, high, spectral_gain)


def mode_matrices(legendre, lat_rows):
    modes, degrees, lats = legendre.shape
    table = legendre.reshape(modes, 1, degrees, lats // lat_rows, 1, lat_rows)
    same = jnp.eye(2, dtype=legendre.dtype).reshape(1, 2, 1, 1, 2, 1)
    low = (table * same).reshape(modes, 2 * degrees, 2 * lats)
    return low, jnp.transpose(low, (0, 2, 1))


def spectral(field, table, low, high, spectral_gain, first_scale, second_scale):
    lat_rows, lon_width, channels = field.shape
    lat_count = lax.axis_size("lat")
    lon_count = lax.axis_size("lon")
    per_device = low.shape[0]
    chunks = chunk_count(per_device)
    partials = jnp.einsum("qp,ipc->qic", table, field, preferred_element_type=jnp.float32)
    partials = (partials * first_scale).astype(jnp.bfloat16)
    partials = partials.reshape(
        chunks, lon_count, lat_count, per_device // chunks, 2 * lat_rows, channels
    )
    coeffs = filter_chain(partials, low, high, spectral_gain)
    coeffs = coeffs.reshape(2 * MODES, lat_rows, channels)
    total = jnp.einsum("qp,qic->ipc", table, coeffs, preferred_element_type=jnp.float32)
    return total * second_scale


def near_matrices(disco_kernel, extents, lat_rows, depth):
    kernel_all = masked_kernel(disco_kernel, extents)
    kernel_own = lax.dynamic_slice_in_dim(
        kernel_all, lax.axis_index("lat") * lat_rows, lat_rows, 0
    )
    span = lat_rows + 2 * depth
    taps = (
        jnp.arange(span, dtype=jnp.int32)[None, :]
        - depth
        - jnp.arange(lat_rows, dtype=jnp.int32)[:, None]
        + MAX_EXT
    )
    picked = (
        jnp.arange(2 * MAX_EXT + 1, dtype=jnp.int32)[None, None, :] == taps[:, :, None]
    ).astype(jnp.float32)
    return jnp.einsum("iwk,ihw->ihk", kernel_own.astype(jnp.float32), picked).astype(jnp.bfloat16)


def window_sum(field, matrices, depth):
    padded = extended(extended(field, (("lat", 0),), depth, False), (("lon", 1),), 1, True)
    lon_width = field.shape[1]
    total = jnp.zeros(field.shape, jnp.float32)
    for shift in range(3):
        total = total + jnp.einsum(
            "ih,hpc->ipc",
            matrices[:, :, shift],
            padded[:, shift : shift + lon_width],
            preferred_element_type=jnp.float32,
        )
    return total


def window_sum_back(field, matrices, depth):
    lat_rows, lon_width, _ = field.shape
    padded = extended(field, (("lon", 1),), 1, True)

    def rows_sum(first, last):
        total = None
        for shift in range(3):
            term = jnp.einsum(
                "ij,ipc->jpc",
                matrices[:, first:last, shift],
                padded[:, 2 - shift : 2 - shift + lon_width],
                preferred_element_type=jnp.float32,
            )
            total = term if total is None else total + term
        return total

    count = lax.axis_size("lat")
    up = [(i, i + 1) for i in range(count - 1)]
    down = [(i + 1, i) for i in range(count - 1)]
    before = rows_sum(0, depth).astype(jnp.bfloat16)
    after = rows_sum(depth + lat_rows, lat_rows + 2 * depth).astype(jnp.bfloat16)
    from_below = lax.ppermute(after, "lat", up)
    from_above = lax.ppermute(before, "lat", down)
    own = rows_sum(depth, depth + lat_rows)
    pad = ((0, lat_rows - depth), (0, 0), (0, 0))
    pad_up = ((lat_rows - depth, 0), (0, 0), (0, 0))
    return (
        own
        + jnp.pad(from_below, pad).astype(jnp.float32)
        + jnp.pad(from_above, pad_up).astype(jnp.float32)
    )


def gelu_slope(values):
    return jax.vjp(jax.nn.gelu, values)[1](jnp.ones_like(values))[0]


def layer(depth, field_in, cotangent, legendre, spectral_gain, disco_kernel, extents, mixing):
    lat_rows, lon_width, channels = field_in.shape
    table = zonal_table(lax.axis_size("lat"), lax.axis_size("lon"), lon_width)
    low, high = mode_matrices(legendre, lat_rows)
    matrices = near_matrices(disco_kernel, extents, lat_rows, depth)
    local_sum = window_sum(field_in, matrices, depth).astype(jnp.bfloat16)
    local_branch = jnp.dot(
        local_sum.reshape(lat_rows * lon_width, channels),
        mixing,
        preferred_element_type=jnp.float32,
    ).reshape(lat_rows, lon_width, channels)
    pre_act = local_branch + spectral(
        field_in, table, low, high, spectral_gain, 1.0 / math.sqrt(NLON), 1.0 / math.sqrt(MODES)
    )
    layer_out = (field_in.astype(jnp.float32) + jax.nn.gelu(pre_act)).astype(jnp.bfloat16)
    upstream = (cotangent.astype(jnp.float32) * gelu_slope(pre_act)).astype(jnp.bfloat16)
    local_back = jnp.dot(
        upstream.reshape(lat_rows * lon_width, channels),
        jnp.transpose(mixing),
        preferred_element_type=jnp.float32,
    )
    local_back = local_back.astype(jnp.bfloat16).reshape(lat_rows, lon_width, channels)
    grad_in = cotangent.astype(jnp.float32) + window_sum_back(local_back, matrices, depth)
    grad_in = grad_in + spectral(
        upstream, table, low, high, spectral_gain, 1.0 / math.sqrt(MODES), 1.0 / math.sqrt(NLON)
    )
    return (layer_out, grad_in.astype(jnp.bfloat16))


NEAR = 2


def body(field_in, cotangent, legendre, spectral_gain, disco_kernel, extents, mixing):
    lat_rows = field_in.shape[0]
    rows = jnp.arange(extents.shape[0], dtype=jnp.int32)
    first = rows // lat_rows * lat_rows
    above = first - jnp.maximum(rows - extents, 0)
    below = jnp.minimum(rows + extents, extents.shape[0] - 1) - (first + lat_rows - 1)
    reach = jnp.max(jnp.maximum(above, below))
    return lax.cond(
        reach <= NEAR,
        functools.partial(layer, NEAR),
        functools.partial(layer, MAX_EXT),
        field_in,
        cotangent,
        legendre,
        spectral_gain,
        disco_kernel,
        extents,
        mixing,
    )


def solution(mesh):
    in_specs = (
        P("lat", "lon", None),
        P("lat", "lon", None),
        P(("lat", "lon"), None, None),
        P(),
        P(),
        P(),
        P(),
    )
    out_specs = (P("lat", "lon", None), P("lat", "lon", None))
    return jax.shard_map(body, mesh=mesh, in_specs=in_specs, out_specs=out_specs, check_vma=False)
```

```python
import functools
import math

import jax
import jax.numpy as jnp
from jax import lax
from jax.experimental import pallas as pl
from jax.experimental.pallas import tpu as pltpu
from jax.sharding import PartitionSpec as P

NLON = 1440
MODES = 256
MAX_EXT = 8


def extended(cells, sides, width, closed):
    for axis, dim in sides:
        count = lax.axis_size(axis)
        ends = count if closed else count - 1
        head = lax.slice_in_dim(cells, 0, width, axis=dim)
        tail = lax.slice_in_dim(cells, cells.shape[dim] - width, cells.shape[dim], axis=dim)
        cells = jnp.concatenate(
            [
                lax.ppermute(tail, axis, [(i, (i + 1) % count) for i in range(ends)]),
                cells,
                lax.ppermute(head, axis, [((i + 1) % count, i) for i in range(ends)]),
            ],
            axis=dim,
        )
    return cells


def masked_kernel(disco_kernel, extents):
    offsets = jnp.arange(2 * MAX_EXT + 1, dtype=jnp.int32) - MAX_EXT
    inside = jnp.abs(offsets)[None, :] <= extents[:, None]
    return jnp.where(inside[:, :, None], disco_kernel, jnp.zeros_like(disco_kernel))


def zonal_tables(mode_numbers, lon_numbers):
    phase = mode_numbers[:, None] * lon_numbers[None, :] % NLON
    angle = phase.astype(jnp.float32) * (2.0 * math.pi / NLON)
    return (jnp.cos(angle).astype(jnp.bfloat16), (-jnp.sin(angle)).astype(jnp.bfloat16))


MESH = pl.DeviceIdType.MESH
GROUP_FLIPS = (0, 2, 1, 3)


CHUNKS = 8


def chunk_count(per_device):
    return CHUNKS if per_device % CHUNKS == 0 else 1


def zonal_table(lat_count, lon_count, lon_width):
    per_device = MODES // lon_count // lat_count
    chunks = chunk_count(per_device)
    width = per_device // chunks
    me = lax.axis_index("lon")
    lon_numbers = me * lon_width + jnp.arange(lon_width, dtype=jnp.int32)
    groups = jnp.array(GROUP_FLIPS, jnp.int32) ^ me
    owners = jnp.arange(lat_count, dtype=jnp.int32)
    modes = (
        (owners[None, None, :, None] * lon_count + groups[None, :, None, None]) * per_device
        + jnp.arange(chunks, dtype=jnp.int32)[:, None, None, None] * width
        + jnp.arange(width, dtype=jnp.int32)[None, None, None, :]
    ).reshape(-1)
    cosines, sines = zonal_tables(modes, lon_numbers)
    return jnp.stack([cosines, sines], axis=1).reshape(2 * MODES, lon_width)


def chain_kernel(
    lat_count, chunks,
    part_ref, table_ref, gain_ref, coef_ref,
    near_buf, far_send, far_buf, own_buf, zonal_buf, value_buf,
    near_sems, far_sems, out_sems, back_sems, edge_sems,
):
    lat = lax.axis_index("lat")
    lon = lax.axis_index("lon")
    near = {"lon": lon ^ 1}
    far = {"lon": lon ^ 2}
    width = part_ref.shape[3]
    rows = part_ref.shape[4]
    channels = part_ref.shape[5]

    def peer(step):
        return lax.rem(lat + step, lat_count)

    barrier = pltpu.get_barrier_semaphore()
    pl.semaphore_signal(barrier, inc=1, device_id=near, device_id_type=MESH)
    pl.semaphore_signal(barrier, inc=1, device_id=far, device_id_type=MESH)

    @pl.loop(1, lat_count)
    def _(step):
        pl.semaphore_signal(barrier, inc=1, device_id={"lat": peer(step)}, device_id_type=MESH)

    pl.semaphore_wait(barrier, lat_count + 1)

    def send(src, dst, sems, index, target):
        return pltpu.make_async_remote_copy(
            src_ref=src,
            dst_ref=dst,
            send_sem=sems.at[(0,) + index],
            recv_sem=sems.at[(1,) + index],
            device_id=target,
            device_id_type=MESH,
        )

    def near_copy(k):
        return send(part_ref.at[k, pl.ds(2, 2)], near_buf.at[k], near_sems, (k,), near)

    def far_copy(k):
        return send(far_send.at[k], far_buf.at[k], far_sems, (k,), far)

    def out_copy(k, step):
        return send(
            own_buf.at[k, peer(step)], zonal_buf.at[k, lat], out_sems, (k, step), {"lat": peer(step)}
        )

    def back_copy(k, step):
        return send(
            value_buf.at[k, peer(step)], coef_ref.at[k, 0, lat], back_sems, (k, step), {"lat": peer(step)}
        )

    def edge_copies(k):
        return (
            send(coef_ref.at[k, 0], coef_ref.at[k, 1], edge_sems, (k, 0), far),
            send(coef_ref.at[k, 0], coef_ref.at[k, 2], edge_sems, (k, 1), near),
            send(coef_ref.at[k, 1], coef_ref.at[k, 3], edge_sems, (k, 2), near),
        )

    for k in range(chunks):
        near_copy(k).start()
    for k in range(chunks):
        near_copy(k).wait_recv()

        @pl.loop(0, lat_count)
        def _(owner):
            got = near_buf[k, 1, owner].astype(jnp.float32)
            far_send[k, owner] = (part_ref[k, 1, owner].astype(jnp.float32) + got).astype(jnp.bfloat16)

        far_copy(k).start()
    for k in range(chunks):
        far_copy(k).wait_recv()

        @pl.loop(0, lat_count)
        def _(owner):
            total = part_ref[k, 0, owner].astype(jnp.float32) + near_buf[k, 0, owner].astype(jnp.float32)
            own_buf[k, owner] = (total + far_buf[k, owner].astype(jnp.float32)).astype(jnp.bfloat16)

        @pl.loop(1, lat_count)
        def _(step):
            out_copy(k, step).start()

        zonal_buf[k, lat] = own_buf[k, lat]
    for k in range(chunks):
        @pl.loop(1, lat_count)
        def _(step):
            out_copy(k, step).wait_recv()

        @pl.loop(0, width)
        def _(mode):
            fields = zonal_buf[k, :, mode].astype(jnp.float32)
            fields = fields.reshape(lat_count, 2, rows // 2, channels)
            table = table_ref[k * width + mode]
            halves = []
            for half in range(2):
                lats = fields[:, half].reshape(lat_count * (rows // 2), channels)
                sums = jnp.dot(table, lats.astype(jnp.bfloat16), preferred_element_type=jnp.float32)
                kept = (sums * gain_ref[...]).astype(jnp.bfloat16)
                values = lax.dot_general(
                    table, kept, (((0,), (0,)), ((), ())), preferred_element_type=jnp.float32
                )
                halves.append(values.reshape(lat_count, 1, rows // 2, channels))
            both = jnp.concatenate(halves, axis=1).reshape(lat_count, rows, channels)
            value_buf[k, :, mode] = both.astype(jnp.bfloat16)

        @pl.loop(1, lat_count)
        def _(step):
            back_copy(k, step).start()

        coef_ref[k, 0, lat] = value_buf[k, lat]
    for k in range(chunks):
        @pl.loop(1, lat_count)
        def _(step):
            back_copy(k, step).wait_recv()

        first, second, _third = edge_copies(k)
        first.start()
        second.start()
    for k in range(chunks):
        first, second, third = edge_copies(k)
        first.wait_recv()
        third.start()
    for k in range(chunks):
        first, second, third = edge_copies(k)
        second.wait_recv()
        third.wait_recv()
        first.wait_send()
        second.wait_send()
        third.wait_send()
        near_copy(k).wait_send()
        far_copy(k).wait_send()

        @pl.loop(1, lat_count)
        def _(step):
            out_copy(k, step).wait_send()
            back_copy(k, step).wait_send()


def filter_chain(partials, legendre, spectral_gain):
    chunks, groups, lat_count, width, rows, channels = partials.shape
    block = (chunks, lat_count, width, rows, channels)
    whole = pl.BlockSpec(memory_space=pltpu.VMEM)
    modes = chunks * width
    return pl.pallas_call(
        functools.partial(chain_kernel, lat_count, chunks),
        out_shape=jax.ShapeDtypeStruct(partials.shape, jnp.bfloat16),
        in_specs=[whole] * 3,
        out_specs=whole,
        scratch_shapes=[
            pltpu.VMEM((chunks, 2, lat_count, width, rows, channels), jnp.bfloat16),
            pltpu.VMEM(block, jnp.bfloat16),
            pltpu.VMEM(block, jnp.bfloat16),
            pltpu.VMEM(block, jnp.bfloat16),
            pltpu.VMEM(block, jnp.bfloat16),
            pltpu.VMEM(block, jnp.bfloat16),
            pltpu.SemaphoreType.DMA((2, chunks)),
            pltpu.SemaphoreType.DMA((2, chunks)),
            pltpu.SemaphoreType.DMA((2, chunks, lat_count)),
            pltpu.SemaphoreType.DMA((2, chunks, lat_count)),
            pltpu.SemaphoreType.DMA((2, chunks, 3)),
        ],
        compiler_params=pltpu.CompilerParams(
            collective_id=0, has_side_effects=True, vmem_limit_bytes=40 * 1024 * 1024
        ),
        cost_estimate=pl.CostEstimate(
            flops=modes * 8 * legendre.shape[1] * legendre.shape[2] * channels,
            bytes_accessed=128 * partials.size,
            transcendentals=0,
        ),
    )(partials, legendre, spectral_gain)


def spectral(field, table, legendre, spectral_gain, first_scale, second_scale, first=()):
    lat_rows, lon_width, channels = field.shape
    lat_count = lax.axis_size("lat")
    lon_count = lax.axis_size("lon")
    per_device = legendre.shape[0]
    chunks = chunk_count(per_device)
    partials = jnp.einsum("qp,ipc->qic", table, field, preferred_element_type=jnp.float32)
    partials = (partials * first_scale).astype(jnp.bfloat16)
    partials = partials.reshape(
        chunks, lon_count, lat_count, per_device // chunks, 2 * lat_rows, channels
    )
    partials, first = lax.optimization_barrier((partials, first))
    coeffs = filter_chain(partials, legendre, spectral_gain)
    coeffs = coeffs.reshape(2 * MODES, lat_rows, channels)
    total = jnp.einsum("qp,qic->ipc", table, coeffs, preferred_element_type=jnp.float32)
    return total * second_scale, first


def near_matrices(disco_kernel, extents, lat_rows, depth):
    kernel_all = masked_kernel(disco_kernel, extents)
    kernel_own = lax.dynamic_slice_in_dim(
        kernel_all, lax.axis_index("lat") * lat_rows, lat_rows, 0
    )
    span = lat_rows + 2 * depth
    taps = (
        jnp.arange(span, dtype=jnp.int32)[None, :]
        - depth
        - jnp.arange(lat_rows, dtype=jnp.int32)[:, None]
        + MAX_EXT
    )
    picked = (
        jnp.arange(2 * MAX_EXT + 1, dtype=jnp.int32)[None, None, :] == taps[:, :, None]
    ).astype(jnp.float32)
    return jnp.einsum("iwk,ihw->ihk", kernel_own.astype(jnp.float32), picked).astype(jnp.bfloat16)


def window_sum(padded, matrices, depth):
    rows = extended(padded, (("lat", 0),), depth, False)
    lon_width = padded.shape[1] - 2
    total = None
    for shift in range(3):
        term = jnp.einsum(
            "ih,hpc->ipc",
            matrices[:, :, shift],
            rows[:, shift : shift + lon_width],
            preferred_element_type=jnp.float32,
        )
        total = term if total is None else total + term
    return total


def rows_back(padded, matrices, first, last):
    lon_width = padded.shape[1] - 2
    total = None
    for shift in range(3):
        term = jnp.einsum(
            "ij,ipc->jpc",
            matrices[:, first:last, shift],
            padded[:, 2 - shift : 2 - shift + lon_width],
            preferred_element_type=jnp.float32,
        )
        total = term if total is None else total + term
    return total


def gelu_slope(values):
    return jax.vjp(jax.nn.gelu, values)[1](jnp.ones_like(values))[0]


def layer(depth, field_in, cotangent, legendre, spectral_gain, disco_kernel, extents, mixing):
    lat_rows, lon_width, channels = field_in.shape
    table = zonal_table(lax.axis_size("lat"), lax.axis_size("lon"), lon_width)
    matrices = near_matrices(disco_kernel, extents, lat_rows, depth)
    padded = extended(field_in, (("lon", 1),), 1, True)
    spectral_part, padded = spectral(
        field_in,
        table,
        legendre,
        spectral_gain,
        1.0 / math.sqrt(NLON),
        1.0 / math.sqrt(MODES),
        padded,
    )
    local_sum = window_sum(padded, matrices, depth).astype(jnp.bfloat16)
    local_branch = jnp.dot(
        local_sum.reshape(lat_rows * lon_width, channels),
        mixing,
        preferred_element_type=jnp.float32,
    ).reshape(lat_rows, lon_width, channels)
    pre_act = local_branch + spectral_part
    layer_out = (field_in.astype(jnp.float32) + jax.nn.gelu(pre_act)).astype(jnp.bfloat16)
    upstream = (cotangent.astype(jnp.float32) * gelu_slope(pre_act)).astype(jnp.bfloat16)
    local_back = jnp.dot(
        upstream.reshape(lat_rows * lon_width, channels),
        jnp.transpose(mixing),
        preferred_element_type=jnp.float32,
    )
    local_back = local_back.astype(jnp.bfloat16).reshape(lat_rows, lon_width, channels)
    padded_back = extended(local_back, (("lon", 1),), 1, True)
    before = rows_back(padded_back, matrices, 0, depth).astype(jnp.bfloat16)
    after = rows_back(padded_back, matrices, depth + lat_rows, lat_rows + 2 * depth)
    after = after.astype(jnp.bfloat16)
    spectral_back, (before, after) = spectral(
        upstream,
        table,
        legendre,
        spectral_gain,
        1.0 / math.sqrt(MODES),
        1.0 / math.sqrt(NLON),
        (before, after),
    )
    count = lax.axis_size("lat")
    from_lower = lax.ppermute(after, "lat", [(i, i + 1) for i in range(count - 1)])
    from_upper = lax.ppermute(before, "lat", [(i + 1, i) for i in range(count - 1)])
    own = rows_back(padded_back, matrices, depth, depth + lat_rows)
    rest = lat_rows - depth
    grad_in = cotangent.astype(jnp.float32) + own
    grad_in = grad_in + jnp.pad(from_lower, ((0, rest), (0, 0), (0, 0))).astype(jnp.float32)
    grad_in = grad_in + jnp.pad(from_upper, ((rest, 0), (0, 0), (0, 0))).astype(jnp.float32)
    grad_in = grad_in + spectral_back
    return (layer_out, grad_in.astype(jnp.bfloat16))


NEAR = 2


def body(field_in, cotangent, legendre, spectral_gain, disco_kernel, extents, mixing):
    lat_rows = field_in.shape[0]
    rows = jnp.arange(extents.shape[0], dtype=jnp.int32)
    first = rows // lat_rows * lat_rows
    above = first - jnp.maximum(rows - extents, 0)
    below = jnp.minimum(rows + extents, extents.shape[0] - 1) - (first + lat_rows - 1)
    reach = jnp.max(jnp.maximum(above, below))
    return lax.cond(
        reach <= NEAR,
        functools.partial(layer, NEAR),
        functools.partial(layer, MAX_EXT),
        field_in,
        cotangent,
        legendre,
        spectral_gain,
        disco_kernel,
        extents,
        mixing,
    )


def solution(mesh):
    in_specs = (
        P("lat", "lon", None),
        P("lat", "lon", None),
        P(("lat", "lon"), None, None),
        P(),
        P(),
        P(),
        P(),
    )
    out_specs = (P("lat", "lon", None), P("lat", "lon", None))
    return jax.shard_map(body, mesh=mesh, in_specs=in_specs, out_specs=out_specs, check_vma=False)
```
